128 devices in a mesh: beam: 16 (over x, z_hi, core), freq: 8 (over z_lo, y).
Axes of the slice: x: 4, y: 4, z: 4 (z_hi: 2, z_lo: 2; z = z_hi * 2 + z_lo), core: 2. Of those that a mesh axis runs over, the one named last changes fastest.
Arguments:
- intensity: bfloat16 [16, 16384, 256], P(None, ('freq', 'beam')), may hold values from -600 to 600, as said below
- channel_mask: int32 [16384], P('freq'), may hold values 0 or 1
- box_widths: int32 [9], replicated, may hold values from 1 to 64
Outputs:
- snr_peak: float32 [16, 4096], P('beam', 'freq')
The draws below stay inside these ranges and needn't reach their ends.
Inputs may be any that keep to these rules, and one draw needn't show every extreme that they name: `intensity`: filterbank intensities of every beam and channel, of any sign.
All inputs are finite; a program needn't handle non-finite values. No bound on the sum of `channel_mask` on one device may be relied on, other than what follows from the above.
Results may differ from the reference program's by a relative error of at most 0.002.
Values may be sent and summed in bfloat16 or wider, within the bound.
No kernel may reach another device: no remote copies, remote signals or barrier semaphores. Data moves between devices by JAX's collectives and lax.ppermute only.
A program may use at most 64 MiB of HBM per device.

```python
import jax
import jax.numpy as jnp
from jax import lax

CHANS = 16384
NDM = 4096
SAMP = 256
NWIDTH = 9
BEAMS = 16


def draw_intensity(key, part):
    key_gain, key_offset, key_noise = jax.random.split(key, 3)
    beam_pos = jnp.arange(BEAMS, dtype=jnp.float32) / max(BEAMS - 1, 1)
    beam_ramp = 3.0 ** beam_pos
    gain_field = beam_ramp[:, None] * jnp.exp(jax.random.uniform(key_gain, (BEAMS, CHANS), jnp.float32, 0.0, 2.302585))
    offsets = jax.random.uniform(key_offset, (BEAMS, CHANS), jnp.float32, -3.0, 3.0) * gain_field
    noise_field = jax.random.normal(key_noise, (BEAMS, CHANS, SAMP), jnp.float32)
    return (offsets[:, :, None] + gain_field[:, :, None] * noise_field).astype(jnp.bfloat16)


def touch_ends(entries, stream_key, low, top_value):
    spot = [jax.random.randint(jax.random.fold_in(stream_key, axis), (), 0, length) for axis, length in enumerate(entries.shape)]
    widest = entries.shape.index(max(entries.shape))
    next_to = spot[:widest] + [(spot[widest] + 1) % entries.shape[widest]] + spot[widest + 1:]
    return entries.at[tuple(spot)].set(low).at[tuple(next_to)].set(top_value)


def setup_inputs(seed: int = 0) -> dict:
    keys = jax.random.split(jax.random.key(seed), 4)
    intensity = draw_intensity(jax.random.fold_in(keys[3], 71), 0)
    channel_mask = touch_ends((jax.random.randint(keys[1], (CHANS,), 0, 8) < 7).astype(jnp.int32), jax.random.fold_in(keys[1], 1), 0, 1)
    box_widths = touch_ends(jax.random.randint(keys[2], (NWIDTH,), 1, 65), jax.random.fold_in(keys[2], 1), 1, 64).astype(jnp.int32)
    return dict(intensity=intensity, channel_mask=channel_mask, box_widths=box_widths)


epsilon = 1e-05

def statistics(channel_sum, squares, channel_mask, row_total):
    channel_mean = channel_sum / row_total
    channel_var = squares / row_total - channel_mean * channel_mean
    channel_scale = lax.rsqrt(channel_var + epsilon) * channel_mask.astype(jnp.float32)
    return (channel_scale, channel_mean)

def advance_ref(row_block, shift_rows):
    samples = row_block.shape[-1]
    padded = jnp.concatenate([row_block, jnp.zeros_like(row_block)], axis=-1)
    time_index = jnp.arange(samples, dtype=jnp.int32)
    gather_index = jnp.minimum(time_index[None, :] + shift_rows[:, None], 2 * samples - 1)
    gather_index = jnp.broadcast_to(gather_index, row_block.shape)
    return jnp.take_along_axis(padded, gather_index, axis=-1)

def dedisperse(band_rows):
    tree_rows = band_rows[:, None, :]
    band_width = 1
    trial_count = 1
    while band_width < CHANS:
        band_width = band_width * 2
        grown = max(1, band_width * NDM // CHANS)
        low_part = tree_rows[0::2]
        high_part = tree_rows[1::2]
        if grown == trial_count:
            tree_rows = low_part + high_part
        else:
            shift_rows = jnp.arange(trial_count, dtype=jnp.int32)
            even_rows = low_part + advance_ref(high_part, shift_rows)
            odd_rows = low_part + advance_ref(high_part, shift_rows + 1)
            tree_rows = jnp.stack([even_rows, odd_rows], axis=2).reshape(low_part.shape[0], 2 * trial_count, SAMP)
        trial_count = grown
    return tree_rows[0]

def boxcar_peaks(series, box_widths):
    samples = series.shape[-1]
    lead_dims = series.shape[:-1]
    prefix = jnp.concatenate([jnp.zeros(lead_dims + (1,), series.dtype), jnp.cumsum(series, axis=-1), jnp.zeros(lead_dims + (samples,), series.dtype)], axis=-1)
    time_index = jnp.arange(samples, dtype=jnp.int32)
    best_peak = None
    for number in range(box_widths.shape[0]):
        box_span = box_widths[number]
        ahead_sum = lax.dynamic_slice_in_dim(prefix, box_span, samples, axis=series.ndim - 1)
        norm_factor = lax.rsqrt((box_span * CHANS).astype(jnp.float32))
        box_sum = (ahead_sum - prefix[..., :samples]) * norm_factor
        box_sum = jnp.where(time_index <= samples - box_span, box_sum, -jnp.inf)
        width_peak = lax.optimization_barrier(jnp.max(box_sum, axis=-1))
        best_peak = width_peak if best_peak is None else jnp.maximum(best_peak, width_peak)
    return best_peak

def reference(intensity, channel_mask, box_widths):
    row_total = float(BEAMS * SAMP)
    channel_sum = lax.optimization_barrier(jnp.sum(intensity.astype(jnp.float32), axis=(0, 2)))
    squares = lax.optimization_barrier(jnp.sum(jnp.square(intensity.astype(jnp.float32)), axis=(0, 2)))
    channel_scale, channel_mean = statistics(channel_sum, squares, channel_mask, row_total)

    def one_beam(beam_rows):
        normed = ((beam_rows.astype(jnp.float32) - channel_mean[:, None]) * channel_scale[:, None]).astype(jnp.bfloat16)
        series = dedisperse(normed.astype(jnp.float32))
        return boxcar_peaks(series, box_widths)
    return lax.map(one_beam, intensity)
```

```python
import functools

import jax
import jax.numpy as jnp
from jax import lax
from jax.experimental import pallas as pl
from jax.experimental.pallas import tpu as pltpu
from jax.sharding import PartitionSpec as P

CHANS = 16384
EPSILON = 1e-05
LANES = 128
CHUNKS = 4


def shifted(first, second, amount, inside):
    first = pltpu.roll(first, amount, 1)
    second = pltpu.roll(second, amount, 1)
    return jnp.where(inside, first, second), jnp.where(inside, second, 0.0)


def channel_kernel(x_hbm, mask_ref, out_ref, xbuf, sems, sums, squares, level2, rows32):
    beams, chans, samples = xbuf.shape
    step = chans // CHUNKS
    copies = []
    for k in range(CHUNKS):
        part = pl.ds(k * step, step)
        copies.append(pltpu.make_async_copy(x_hbm.at[:, part, :], xbuf.at[:, part, :], sems.at[k]))
        copies[-1].start()
    for k in range(CHUNKS):
        copies[k].wait()
        for c in range(k * step, (k + 1) * step, 16):
            total = square = None
            for b in range(beams):
                v = xbuf[b, c : c + 16, :].astype(jnp.float32)
                total = v if total is None else total + v
                square = v * v if square is None else square + v * v
            sums[c : c + 16, :] = total[:, :LANES] + total[:, LANES:]
            squares[c : c + 16, :] = square[:, :LANES] + square[:, LANES:]
    count = float(beams * samples)
    mean = jnp.sum(sums[...].T, axis=0, keepdims=True) / count
    var = jnp.sum(squares[...].T, axis=0, keepdims=True) / count - mean * mean
    mask = mask_ref[pl.ds(lax.axis_index("beam"), 1), :].astype(jnp.float32)
    scale = lax.rsqrt(var + EPSILON) * mask
    bands = chans // 4
    row = lax.broadcasted_iota(jnp.int32, (bands, chans), 0)
    chan = lax.broadcasted_iota(jnp.int32, (bands, chans), 1)
    weight = jnp.where(chan // 4 == row, scale, 0.0)
    high = weight.astype(jnp.bfloat16)
    rest = (weight - high.astype(jnp.float32)).astype(jnp.bfloat16)
    held = high.astype(jnp.float32) + rest.astype(jnp.float32)
    offset = jnp.sum(held * mean, axis=1, keepdims=True)
    both = jnp.concatenate([high, rest], axis=0)
    for b in range(beams):
        y = jnp.dot(both, xbuf[b], preferred_element_type=jnp.float32)
        y = y[:bands] + y[bands:] - offset
        level2[0, b * bands : (b + 1) * bands, :] = y[:, :LANES]
        level2[1, b * bands : (b + 1) * bands, :] = y[:, LANES:]
    lane = lax.broadcasted_iota(jnp.int32, (8, LANES), 1)

    def subband(tile, level, s):
        if level == 2:
            at = pl.ds(tile * 8 * bands + s, 8, stride=bands)
            return [(level2[0, at, :], level2[1, at, :])]
        low = subband(tile, level - 1, 2 * s)
        high = subband(tile, level - 1, 2 * s + 1)
        rows = []
        for r in range(len(low)):
            for shift in (r, r + 1):
                moved = high[r]
                if shift:
                    moved = shifted(*high[r], LANES - shift, lane < LANES - shift)
                rows.append((low[r][0] + moved[0], low[r][1] + moved[1]))
        return rows

    for tile in range(beams // 8):
        rows = subband(tile, 7, 0)
        for r, halves in enumerate(rows):
            for h in range(2):
                start = ((r // 4) * beams + tile * 8) * 8 + (r % 4) * 2 + h
                rows32[pl.ds(start, 8, stride=8), :] = halves[h]
    out_ref[...] = rows32[...].astype(jnp.bfloat16)


def trial_kernel(rows_ref, widths_ref, out_ref, rows32, level11, trials, prefix):
    f = lax.axis_index("freq")
    rows32[...] = rows_ref[...].astype(jnp.float32)
    lane = lax.broadcasted_iota(jnp.int32, (8, LANES), 1)
    sub = lax.broadcasted_iota(jnp.int32, (8, LANES), 0)
    zero = jnp.zeros((8, LANES), jnp.float32)

    bands = []
    for u in range(16):
        bands.append([
            tuple(rows32[pl.ds(u * 8 + i * 2 + h, 8, stride=128), :] for h in range(2)) for i in range(4)
        ])
    parents = 4
    while len(bands) > 1:
        base = f * parents
        late = None
        if len(bands) == 2:
            late = base >= LANES
            base = jnp.where(late, base - LANES, base)
        moves = []
        for i in range(parents + 1):
            s = base + i
            moves.append(((LANES - s) & (LANES - 1), lane < LANES - s))
        merged = []
        for low, high in zip(bands[0::2], bands[1::2]):
            out = []
            for i in range(parents):
                first, second = high[i]
                if late is not None:
                    first = jnp.where(late, second, first)
                    second = jnp.where(late, zero, second)
                for amount, inside in (moves[i], moves[i + 1]):
                    a, b = shifted(first, second, amount, inside)
                    out.append((low[i][0] + a, low[i][1] + b))
            merged.append(out)
        bands = merged
        parents *= 2
    for j in range(parents):
        first, second = bands[0][j]
        for bit in range(3):
            s = (f * parents + j) << bit
            q = s // LANES
            a = jnp.where(q == 0, first, jnp.where(q == 1, second, zero))
            b = jnp.where(q == 0, second, zero)
            s = s & (LANES - 1)
            a, b = shifted(a, b, (LANES - s) & (LANES - 1), lane < LANES - s)
            chosen = (sub >> bit & 1) == 1
            first = jnp.where(chosen, a, first)
            second = jnp.where(chosen, b, second)
        level11[0, j * 8 : j * 8 + 8, :] = first
        level11[1, j * 8 : j * 8 + 8, :] = second

    def ahead(pair, s):
        return shifted(*pair, LANES - s, lane < LANES - s) if s else pair

    def added(low, high):
        return low[0] + high[0], low[1] + high[1]

    for jt in range(8):
        tiles = []
        for band in range(8):
            at = pl.ds(jt * 64 + band, 8, stride=8)
            tiles.append((level11[0, at, :], level11[1, at, :]))
        l12 = [[added(tiles[2 * k], ahead(tiles[2 * k + 1], e)) for e in range(2)] for k in range(4)]
        l13 = [
            [added(l12[2 * k][e >> 1], ahead(l12[2 * k + 1][e >> 1], (e + 1) // 2)) for e in range(4)]
            for k in range(2)
        ]
        for c in range(8):
            pair = added(l13[0][c >> 1], ahead(l13[1][c >> 1], (c + 1) // 2))
            at = pl.ds(jt * 64 + c, 8, stride=8)
            for h in range(2):
                trials[h, at, :] = pair[h]

    count = trials.shape[1]
    samples = 2 * LANES
    top = prefix.shape[1]
    parts = []
    for h in range(2):
        d = trials[h]
        high = d.astype(jnp.bfloat16)
        parts.append((high, (d - high.astype(jnp.float32)).astype(jnp.bfloat16)))
    values = jnp.concatenate([parts[0][0], parts[1][0], parts[0][1], parts[1][1]], axis=1)
    size = (samples + 16, 4 * LANES)
    step = lax.broadcasted_iota(jnp.int32, size, 0)
    time = lax.broadcasted_iota(jnp.int32, size, 1) & (samples - 1)
    lower = jnp.where(time < step, 1.0, 0.0).astype(jnp.bfloat16)
    summed = lax.dot_general(lower, values, (((1,), (1,)), ((), ())), preferred_element_type=jnp.float32)
    for lt in range(count // LANES):
        prefix[lt, : samples + 8, :] = summed[: samples + 8, lt * LANES : (lt + 1) * LANES]
        prefix[lt, samples : samples + 8, :] = jnp.where(
            sub == 0, summed[samples : samples + 8, lt * LANES : (lt + 1) * LANES], -jnp.inf
        )
        prefix[lt, samples + 8 :, :] = jnp.full((top - samples - 8, LANES), -jnp.inf, jnp.float32)
    for lt in range(count // LANES):
        starts = [prefix[lt, t : t + 8, :] for t in range(0, samples, 8)]
        best = None
        for k in range(widths_ref.shape[0]):
            w = widths_ref[k]
            peak = None
            for n, start in enumerate(starts):
                box = prefix[lt, pl.ds(8 * n + w, 8), :] - start
                peak = box if peak is None else jnp.maximum(peak, box)
            peak = peak * lax.rsqrt(jnp.full((8, LANES), w * CHANS, jnp.int32).astype(jnp.float32))
            best = peak if best is None else jnp.maximum(best, peak)
        out_ref[:, lt * LANES : (lt + 1) * LANES] = jnp.max(best, axis=0, keepdims=True)


def shards(intensity, channel_mask, box_widths):
    beams, chans, samples = intensity.shape
    devices = lax.axis_size("beam") * lax.axis_size("freq")
    rows = pl.pallas_call(
        channel_kernel,
        out_shape=jax.ShapeDtypeStruct((devices * 8, LANES), jnp.bfloat16),
        in_specs=[pl.BlockSpec(memory_space=pl.ANY), pl.BlockSpec(memory_space=pltpu.VMEM)],
        out_specs=pl.BlockSpec(memory_space=pltpu.VMEM),
        scratch_shapes=[
            pltpu.VMEM((beams, chans, samples), jnp.bfloat16),
            pltpu.SemaphoreType.DMA((CHUNKS,)),
            pltpu.VMEM((chans, LANES), jnp.float32),
            pltpu.VMEM((chans, LANES), jnp.float32),
            pltpu.VMEM((2, beams * chans // 4, LANES), jnp.float32),
            pltpu.VMEM((devices * 8, LANES), jnp.float32),
        ],
        compiler_params=pltpu.CompilerParams(vmem_limit_bytes=32 * 1024 * 1024),
        name="channel_levels",
    )(intensity, channel_mask.reshape(-1, LANES))
    rows = lax.all_to_all(rows.reshape(devices, 8, LANES), ("freq", "beam"), 0, 0, tiled=True)
    return pl.pallas_call(
        trial_kernel,
        out_shape=jax.ShapeDtypeStruct((1, 4 * LANES), jnp.float32),
        in_specs=[pl.BlockSpec(memory_space=pltpu.VMEM), pl.BlockSpec(memory_space=pltpu.SMEM)],
        out_specs=pl.BlockSpec(memory_space=pltpu.VMEM),
        scratch_shapes=[
            pltpu.VMEM((devices * 8, LANES), jnp.float32),
            pltpu.VMEM((2, 512, LANES), jnp.float32),
            pltpu.VMEM((2, 512, LANES), jnp.float32),
            pltpu.VMEM((4, 2 * LANES + 72, LANES), jnp.float32),
        ],
        compiler_params=pltpu.CompilerParams(vmem_limit_bytes=32 * 1024 * 1024),
        name="trial_levels",
    )(rows.reshape(devices * 8, LANES), box_widths)


def solution(mesh):
    in_specs = (P(None, ("freq", "beam"), None), P("freq"), P())
    out_specs = P("beam", "freq")
    return jax.shard_map(shards, mesh=mesh, in_specs=in_specs, out_specs=out_specs, check_vma=False)
```

```python
import functools

import jax
import jax.numpy as jnp
from jax import lax
from jax.experimental import pallas as pl
from jax.experimental.pallas import tpu as pltpu
from jax.sharding import PartitionSpec as P

CHANS = 16384
EPSILON = 1e-05
LANES = 128
CHUNKS = 4
SKEW = 16
TAIL = 4


def shifted(first, second, amount, inside):
    first = pltpu.roll(first, amount, 1)
    second = pltpu.roll(second, amount, 1)
    return jnp.where(inside, first, second), jnp.where(inside, second, 0.0)


def channel_kernel(x_hbm, mask_hbm, out_ref, xbuf, masks, sems, sums, squares, level2, rows32):
    beams, chans, samples = xbuf.shape
    step = chans // CHUNKS
    copies = []
    for k in range(CHUNKS):
        part = pl.ds(k * step, step)
        copies.append(pltpu.make_async_copy(x_hbm.at[:, part, :], xbuf.at[:, part, :], sems.at[k]))
        copies[-1].start()
    copies.append(pltpu.make_async_copy(mask_hbm, masks, sems.at[CHUNKS]))
    copies[-1].start()
    for k in range(CHUNKS):
        copies[k].wait()
        for c in range(k * step, (k + 1) * step, 16):
            total = square = None
            for b in range(beams):
                v = xbuf[b, c : c + 16, :].astype(jnp.float32)
                total = v if total is None else total + v
                square = v * v if square is None else square + v * v
            sums[c : c + 16, :] = total[:, :LANES] + total[:, LANES:]
            squares[c : c + 16, :] = square[:, :LANES] + square[:, LANES:]
    count = float(beams * samples)
    mean = jnp.sum(sums[...].T, axis=0, keepdims=True) / count
    var = jnp.sum(squares[...].T, axis=0, keepdims=True) / count - mean * mean
    copies[CHUNKS].wait()
    mask = masks[pl.ds(lax.axis_index("beam"), 1), :].astype(jnp.float32)
    scale = lax.rsqrt(var + EPSILON) * mask
    bands = chans // 4
    row = lax.broadcasted_iota(jnp.int32, (bands, chans), 0)
    chan = lax.broadcasted_iota(jnp.int32, (bands, chans), 1)
    weight = jnp.where(chan // 4 == row, scale, 0.0)
    high = weight.astype(jnp.bfloat16)
    rest = (weight - high.astype(jnp.float32)).astype(jnp.bfloat16)
    held = high.astype(jnp.float32) + rest.astype(jnp.float32)
    offset = jnp.sum(held * mean, axis=1, keepdims=True)
    both = jnp.concatenate([high, rest], axis=0)
    for b in range(beams):
        y = jnp.dot(both, xbuf[b], preferred_element_type=jnp.float32)
        y = y[:bands] + y[bands:] - offset
        level2[0, b * bands : (b + 1) * bands, :] = y[:, :LANES]
        level2[1, b * bands : (b + 1) * bands, :] = y[:, LANES:]
    lane = lax.broadcasted_iota(jnp.int32, (8, LANES), 1)

    def subband(tile, level, s):
        if level == 2:
            at = pl.ds(tile * 8 * bands + s, 8, stride=bands)
            return [(level2[0, at, :], level2[1, at, :])]
        low = subband(tile, level - 1, 2 * s)
        high = subband(tile, level - 1, 2 * s + 1)
        rows = []
        for r in range(len(low)):
            for shift in (r, r + 1):
                moved = high[r]
                if shift:
                    moved = shifted(*high[r], LANES - shift, lane < LANES - shift)
                rows.append((low[r][0] + moved[0], low[r][1] + moved[1]))
        return rows

    for tile in range(beams // 8):
        rows = subband(tile, 7, 0)
        for r, halves in enumerate(rows):
            for h in range(2):
                start = ((r // 4) * beams + tile * 8) * 8 + (r % 4) * 2 + h
                rows32[pl.ds(start, 8, stride=8), :] = halves[h]
    out_ref[...] = rows32[...].astype(jnp.bfloat16)


def trial_kernel(rows_ref, widths_hbm, out_ref, widths, sem, rows32, level11, skewed, trials, prefix):
    copy = pltpu.make_async_copy(widths_hbm, widths, sem)
    copy.start()
    f = lax.axis_index("freq")
    rows32[...] = rows_ref[...].astype(jnp.float32)
    lane = lax.broadcasted_iota(jnp.int32, (8, LANES), 1)
    sub = lax.broadcasted_iota(jnp.int32, (8, LANES), 0)
    zero = jnp.zeros((8, LANES), jnp.float32)

    bands = []
    for u in range(16):
        bands.append([
            tuple(rows32[pl.ds(u * 8 + i * 2 + h, 8, stride=128), :] for h in range(2)) for i in range(4)
        ])
    parents = 4
    while len(bands) > 1:
        base = f * parents
        late = None
        if len(bands) == 2:
            late = base >= LANES
            base = jnp.where(late, base - LANES, base)
        moves = []
        for i in range(parents + 1):
            s = base + i
            moves.append(((LANES - s) & (LANES - 1), lane < LANES - s))
        merged = []
        for low, high in zip(bands[0::2], bands[1::2]):
            out = []
            for i in range(parents):
                first, second = high[i]
                if late is not None:
                    first = jnp.where(late, second, first)
                    second = jnp.where(late, zero, second)
                for amount, inside in (moves[i], moves[i + 1]):
                    a, b = shifted(first, second, amount, inside)
                    out.append((low[i][0] + a, low[i][1] + b))
            merged.append(out)
        bands = merged
        parents *= 2
    for j in range(parents):
        for h in range(2):
            level11[h, j * 8 : j * 8 + 8, :] = bands[0][j][h]

    def skew(block, carry):
        for n in range(SKEW):
            j = block * SKEW + n
            at = pl.ds(pl.multiple_of(j * 8, 8), 8)
            first, second = level11[0, at, :], level11[1, at, :]
            time = lane + sub * (f * parents + j)
            moved = time & (LANES - 1)
            first = jnp.take_along_axis(first, moved, axis=1, mode="promise_in_bounds")
            second = jnp.take_along_axis(second, moved, axis=1, mode="promise_in_bounds")
            inside = time < LANES
            first = jnp.where(inside, first, jnp.where(time < 2 * LANES, second, 0.0))
            second = jnp.where(inside, second, 0.0)
            skewed[0, at, :] = first
            skewed[1, at, :] = second
        return carry

    lax.fori_loop(0, parents // SKEW, skew, 0)

    def ahead(pair, s):
        return shifted(*pair, LANES - s, lane < LANES - s) if s else pair

    def added(low, high):
        return low[0] + high[0], low[1] + high[1]

    def last_levels(block, carry):
        for n in range(TAIL):
            last_tile(block * TAIL + n)
        return carry

    def last_tile(jt):
        tiles = []
        for band in range(8):
            at = pl.ds(jt * 64 + band, 8, stride=8)
            tiles.append((skewed[0, at, :], skewed[1, at, :]))
        l12 = [[added(tiles[2 * k], ahead(tiles[2 * k + 1], e)) for e in range(2)] for k in range(4)]
        l13 = [
            [added(l12[2 * k][e >> 1], ahead(l12[2 * k + 1][e >> 1], (e + 1) // 2)) for e in range(4)]
            for k in range(2)
        ]
        for c in range(8):
            pair = added(l13[0][c >> 1], ahead(l13[1][c >> 1], (c + 1) // 2))
            at = pl.ds(jt * 64 + c, 8, stride=8)
            for h in range(2):
                trials[h, at, :] = pair[h]

    lax.fori_loop(0, 8 // TAIL, last_levels, 0)

    count = trials.shape[1]
    samples = 2 * LANES
    top = prefix.shape[1]
    parts = []
    for h in range(2):
        d = trials[h]
        high = d.astype(jnp.bfloat16)
        parts.append((high, (d - high.astype(jnp.float32)).astype(jnp.bfloat16)))
    values = jnp.concatenate([parts[0][0], parts[1][0], parts[0][1], parts[1][1]], axis=1)
    size = (samples + 16, 4 * LANES)
    step = lax.broadcasted_iota(jnp.int32, size, 0)
    time = lax.broadcasted_iota(jnp.int32, size, 1) & (samples - 1)
    lower = jnp.where(time < step, 1.0, 0.0).astype(jnp.bfloat16)
    summed = lax.dot_general(lower, values, (((1,), (1,)), ((), ())), preferred_element_type=jnp.float32)
    for lt in range(count // LANES):
        prefix[lt, : samples + 8, :] = summed[: samples + 8, lt * LANES : (lt + 1) * LANES]
        prefix[lt, samples : samples + 8, :] = jnp.where(
            sub == 0, summed[samples : samples + 8, lt * LANES : (lt + 1) * LANES], -jnp.inf
        )
        prefix[lt, samples + 8 :, :] = jnp.full((top - samples - 8, LANES), -jnp.inf, jnp.float32)
    copy.wait()
    for lt in range(count // LANES):
        starts = [prefix[lt, t : t + 8, :] for t in range(0, samples, 8)]
        best = None
        for k in range(widths.shape[0]):
            w = widths[k]
            peak = None
            for n, start in enumerate(starts):
                box = prefix[lt, pl.ds(8 * n + w, 8), :] - start
                peak = box if peak is None else jnp.maximum(peak, box)
            peak = peak * lax.rsqrt(jnp.full((8, LANES), w * CHANS, jnp.int32).astype(jnp.float32))
            best = peak if best is None else jnp.maximum(best, peak)
        out_ref[:, lt * LANES : (lt + 1) * LANES] = jnp.max(best, axis=0, keepdims=True)


def in_hbm(array):
    return pltpu.with_memory_space_constraint(array, pltpu.HBM)


def shards(intensity, channel_mask, box_widths):
    beams, chans, samples = intensity.shape
    devices = lax.axis_size("beam") * lax.axis_size("freq")
    rows = pl.pallas_call(
        channel_kernel,
        out_shape=jax.ShapeDtypeStruct((devices * 8, LANES), jnp.bfloat16),
        in_specs=[pl.BlockSpec(memory_space=pltpu.HBM), pl.BlockSpec(memory_space=pltpu.HBM)],
        out_specs=pl.BlockSpec(memory_space=pltpu.VMEM),
        scratch_shapes=[
            pltpu.VMEM((beams, chans, samples), jnp.bfloat16),
            pltpu.VMEM((chans * lax.axis_size("beam") // LANES, LANES), jnp.int32),
            pltpu.SemaphoreType.DMA((CHUNKS + 1,)),
            pltpu.VMEM((chans, LANES), jnp.float32),
            pltpu.VMEM((chans, LANES), jnp.float32),
            pltpu.VMEM((2, beams * chans // 4, LANES), jnp.float32),
            pltpu.VMEM((devices * 8, LANES), jnp.float32),
        ],
        compiler_params=pltpu.CompilerParams(vmem_limit_bytes=32 * 1024 * 1024),
        name="channel_levels",
    )(in_hbm(intensity), in_hbm(channel_mask.reshape(-1, LANES)))
    rows = lax.all_to_all(rows.reshape(devices, 8, LANES), ("freq", "beam"), 0, 0, tiled=True)
    return pl.pallas_call(
        trial_kernel,
        out_shape=jax.ShapeDtypeStruct((1, 4 * LANES), jnp.float32),
        in_specs=[pl.BlockSpec(memory_space=pltpu.VMEM), pl.BlockSpec(memory_space=pltpu.HBM)],
        out_specs=pl.BlockSpec(memory_space=pltpu.VMEM),
        scratch_shapes=[
            pltpu.SMEM(box_widths.shape, jnp.int32),
            pltpu.SemaphoreType.DMA,
            pltpu.VMEM((devices * 8, LANES), jnp.float32),
            pltpu.VMEM((2, 512, LANES), jnp.float32),
            pltpu.VMEM((2, 512, LANES), jnp.float32),
            pltpu.VMEM((2, 512, LANES), jnp.float32),
            pltpu.VMEM((4, 2 * LANES + 72, LANES), jnp.float32),
        ],
        compiler_params=pltpu.CompilerParams(vmem_limit_bytes=32 * 1024 * 1024),
        name="trial_levels",
    )(rows.reshape(devices * 8, LANES), in_hbm(box_widths))


def solution(mesh):
    in_specs = (P(None, ("freq", "beam"), None), P("freq"), P())
    out_specs = P("beam", "freq")
    return jax.shard_map(shards, mesh=mesh, in_specs=in_specs, out_specs=out_specs, check_vma=False)
```

```python
import functools

import jax
import jax.numpy as jnp
from jax import lax
from jax.experimental import pallas as pl
from jax.experimental.pallas import tpu as pltpu
from jax.sharding import PartitionSpec as P

CHANS = 16384
EPSILON = 1e-05
LANES = 128
CHUNKS = 4
WIDTHS = 9


def shifted(first, second, amount, inside):
    first = pltpu.roll(first, amount, 1)
    second = pltpu.roll(second, amount, 1)
    return jnp.where(inside, first, second), jnp.where(inside, second, 0.0)


def channel_kernel(x_hbm, mask_hbm, out_ref, xbuf, masks, sems, sums, squares, level2, rows32):
    beams, chans, samples = xbuf.shape
    step = chans // CHUNKS
    copies = []
    for k in range(CHUNKS):
        part = pl.ds(k * step, step)
        copies.append(pltpu.make_async_copy(x_hbm.at[:, part, :], xbuf.at[:, part, :], sems.at[k]))
        copies[-1].start()
    copies.append(pltpu.make_async_copy(mask_hbm, masks, sems.at[CHUNKS]))
    copies[-1].start()
    for k in range(CHUNKS):
        copies[k].wait()
        for c in range(k * step, (k + 1) * step, 16):
            total = square = None
            for b in range(beams):
                v = xbuf[b, c : c + 16, :].astype(jnp.float32)
                total = v if total is None else total + v
                square = v * v if square is None else square + v * v
            sums[c : c + 16, :] = total[:, :LANES] + total[:, LANES:]
            squares[c : c + 16, :] = square[:, :LANES] + square[:, LANES:]
    count = float(beams * samples)
    mean = jnp.sum(sums[...].T, axis=0, keepdims=True) / count
    var = jnp.sum(squares[...].T, axis=0, keepdims=True) / count - mean * mean
    copies[CHUNKS].wait()
    mask = masks[pl.ds(lax.axis_index("beam"), 1), :].astype(jnp.float32)
    scale = lax.rsqrt(var + EPSILON) * mask
    bands = chans // 4
    row = lax.broadcasted_iota(jnp.int32, (bands, chans), 0)
    chan = lax.broadcasted_iota(jnp.int32, (bands, chans), 1)
    weight = jnp.where(chan // 4 == row, scale, 0.0)
    high = weight.astype(jnp.bfloat16)
    rest = (weight - high.astype(jnp.float32)).astype(jnp.bfloat16)
    held = high.astype(jnp.float32) + rest.astype(jnp.float32)
    offset = jnp.sum(held * mean, axis=1, keepdims=True)
    both = jnp.concatenate([high, rest], axis=0)
    for b in range(beams):
        y = jnp.dot(both, xbuf[b], preferred_element_type=jnp.float32)
        y = y[:bands] + y[bands:] - offset
        level2[0, b * bands : (b + 1) * bands, :] = y[:, :LANES]
        level2[1, b * bands : (b + 1) * bands, :] = y[:, LANES:]
    lane = lax.broadcasted_iota(jnp.int32, (8, LANES), 1)

    def subband(tile, level, s):
        if level == 2:
            at = pl.ds(tile * 8 * bands + s, 8, stride=bands)
            return [(level2[0, at, :], level2[1, at, :])]
        low = subband(tile, level - 1, 2 * s)
        high = subband(tile, level - 1, 2 * s + 1)
        rows = []
        for r in range(len(low)):
            for shift in (r, r + 1):
                moved = high[r]
                if shift:
                    moved = shifted(*high[r], LANES - shift, lane < LANES - shift)
                rows.append((low[r][0] + moved[0], low[r][1] + moved[1]))
        return rows

    for tile in range(beams // 8):
        rows = subband(tile, 7, 0)
        for r, halves in enumerate(rows):
            for h in range(2):
                start = ((r // 4) * beams + tile * 8) * 8 + h * 4 + r % 4
                rows32[pl.ds(start, 8, stride=8), :] = halves[h]
    out_ref[...] = rows32[...].astype(jnp.bfloat16)


def trial_kernel(rows_ref, widths_hbm, out_ref, widths, sem, rows32, level11, trials, prefix):
    copy = pltpu.make_async_copy(widths_hbm, widths, sem)
    copy.start()
    f = lax.axis_index("freq")
    rows32[...] = rows_ref[...].astype(jnp.float32)
    lane = lax.broadcasted_iota(jnp.int32, (8, LANES), 1)
    sub = lax.broadcasted_iota(jnp.int32, (8, LANES), 0)
    upper = sub >= 4
    row = sub & 3

    pace = f * 4 + row
    begin = lane + jnp.where(upper, 64 * pace, 0)
    rows = []
    for u in range(64):
        here, there = u * 8, (u + 64) * 8
        first = jnp.where(upper, rows32[there - 4 : there + 4, :], rows32[here : here + 8, :])
        second = jnp.where(upper, rows32[there : there + 8, :], rows32[here + 4 : here + 12, :])
        time, begin = begin, begin + pace
        moved = time & (LANES - 1)
        inside = time < LANES
        first = jnp.take_along_axis(first, moved, axis=1, mode="promise_in_bounds")
        second = jnp.take_along_axis(second, moved, axis=1, mode="promise_in_bounds")
        first = jnp.where(inside, first, jnp.where(time < 2 * LANES, second, 0.0))
        rows.append((first, jnp.where(inside, second, 0.0)))

    def ahead(pair, s):
        return shifted(*pair, LANES - s, lane < LANES - s) if s else pair

    for k in range(6):
        width = 1 << k
        grown = []
        for u in range(32 >> k):
            for c in range(width):
                low = rows[2 * u * width + c]
                high = rows[2 * u * width + c + width]
                for e in range(2):
                    moved = ahead(high, c + e)
                    grown.append((low[0] + moved[0], low[1] + moved[1]))
        rows = grown
        if k == 3:
            for n, pair in enumerate(rows):
                for h in range(2):
                    level11[h, n * 8 : n * 8 + 8, :] = pair[h]
            rows = [tuple(level11[h, n * 8 : n * 8 + 8, :] for h in range(2)) for n in range(64)]

    for c in range(64):
        halves = [rows[c][h] for h in range(2)]
        turned = [pltpu.roll(v, 4, 0) for v in halves]
        pair = [jnp.where(upper, v, t) for v, t in zip(halves, turned)]
        even, odd = ahead(pair, c), ahead(pair, c + 1)
        for h in range(2):
            low = jnp.where(upper, turned[h], halves[h])
            trials[h, c * 8 : c * 8 + 8, :] = low + jnp.where(upper, odd[h], even[h])

    count = trials.shape[1]
    samples = 2 * LANES
    span = prefix.shape[0] // 8
    parts = []
    for h in range(2):
        d = trials[h]
        high = d.astype(jnp.bfloat16)
        parts.append((high, (d - high.astype(jnp.float32)).astype(jnp.bfloat16)))
    values = jnp.concatenate([parts[0][0], parts[1][0], parts[0][1], parts[1][1]], axis=1)
    size = (samples + 16, 4 * LANES)
    step = lax.broadcasted_iota(jnp.int32, size, 0)
    time = lax.broadcasted_iota(jnp.int32, size, 1) & (samples - 1)
    lower = jnp.where(time < step, 1.0, 0.0).astype(jnp.bfloat16)
    summed = lax.dot_general(lower, values, (((1,), (1,)), ((), ())), preferred_element_type=jnp.float32)
    least = jnp.full((8, LANES), -jnp.inf, jnp.float32)
    for tile in range(count // LANES):
        for t in range(0, samples + 64, 8):
            part = least
            if t <= samples:
                part = summed[t : t + 8, tile * LANES : (tile + 1) * LANES]
            if t == samples:
                part = jnp.where(sub == 0, part, least)
            if t < span:
                prefix[pl.ds(t * 8 + tile, 8, stride=8), :] = part
            if t >= LANES:
                prefix[pl.ds((t - LANES) * 8 + 4 + tile, 8, stride=8), :] = part
    copy.wait()

    def boxcars(block, peaks):
        base = pl.multiple_of(block * 256, 256)
        starts = [prefix[pl.ds(base + t * 8, 8), :] for t in range(32)]
        out = []
        for k in range(WIDTHS):
            w = pl.multiple_of(base + widths[k] * 8, 8)
            two = [peaks[k], None]
            for n, start in enumerate(starts):
                box = prefix[pl.ds(w + n * 8, 8), :] - start
                two[n % 2] = box if two[n % 2] is None else jnp.maximum(two[n % 2], box)
            out.append(jnp.maximum(*two))
        return tuple(out)

    peaks = lax.fori_loop(0, 4, boxcars, (least,) * WIDTHS)
    best = least
    for k in range(WIDTHS):
        norm = lax.rsqrt(jnp.full((8, LANES), widths[k] * CHANS, jnp.int32).astype(jnp.float32))
        best = jnp.maximum(best, peaks[k] * norm)
    best = jnp.maximum(best, pltpu.roll(best, 4, 0))
    for i in range(count // LANES):
        place = (lane >> 1) * 8 + (lane & 1) * 4 + i
        found = jnp.take_along_axis(best, place & (LANES - 1), axis=1, mode="promise_in_bounds")
        found = jnp.where(sub == place // LANES, found, least)
        out_ref[:, i * LANES : (i + 1) * LANES] = jnp.max(found, axis=0, keepdims=True)


def in_hbm(array):
    return pltpu.with_memory_space_constraint(array, pltpu.HBM)


def shards(intensity, channel_mask, box_widths):
    beams, chans, samples = intensity.shape
    devices = lax.axis_size("beam") * lax.axis_size("freq")
    rows = pl.pallas_call(
        channel_kernel,
        out_shape=jax.ShapeDtypeStruct((devices * 8, LANES), jnp.bfloat16),
        in_specs=[pl.BlockSpec(memory_space=pltpu.HBM), pl.BlockSpec(memory_space=pltpu.HBM)],
        out_specs=pl.BlockSpec(memory_space=pltpu.VMEM),
        scratch_shapes=[
            pltpu.VMEM((beams, chans, samples), jnp.bfloat16),
            pltpu.VMEM((chans * lax.axis_size("beam") // LANES, LANES), jnp.int32),
            pltpu.SemaphoreType.DMA((CHUNKS + 1,)),
            pltpu.VMEM((chans, LANES), jnp.float32),
            pltpu.VMEM((chans, LANES), jnp.float32),
            pltpu.VMEM((2, beams * chans // 4, LANES), jnp.float32),
            pltpu.VMEM((devices * 8, LANES), jnp.float32),
        ],
        compiler_params=pltpu.CompilerParams(vmem_limit_bytes=32 * 1024 * 1024),
        name="channel_levels",
    )(in_hbm(intensity), in_hbm(channel_mask.reshape(-1, LANES)))
    rows = lax.all_to_all(rows.reshape(devices, 8, LANES), ("freq", "beam"), 0, 0, tiled=True)
    return pl.pallas_call(
        trial_kernel,
        out_shape=jax.ShapeDtypeStruct((1, 4 * LANES), jnp.float32),
        in_specs=[pl.BlockSpec(memory_space=pltpu.VMEM), pl.BlockSpec(memory_space=pltpu.HBM)],
        out_specs=pl.BlockSpec(memory_space=pltpu.VMEM),
        scratch_shapes=[
            pltpu.SMEM(box_widths.shape, jnp.int32),
            pltpu.SemaphoreType.DMA,
            pltpu.VMEM((devices * 8, LANES), jnp.float32),
            pltpu.VMEM((2, 512, LANES), jnp.float32),
            pltpu.VMEM((2, 512, LANES), jnp.float32),
            pltpu.VMEM((8 * (LANES + 64), LANES), jnp.float32),
        ],
        compiler_params=pltpu.CompilerParams(vmem_limit_bytes=32 * 1024 * 1024),
        name="trial_levels",
    )(rows.reshape(devices * 8, LANES), in_hbm(box_widths))


def solution(mesh):
    in_specs = (P(None, ("freq", "beam"), None), P("freq"), P())
    out_specs = P("beam", "freq")
    return jax.shard_map(shards, mesh=mesh, in_specs=in_specs, out_specs=out_specs, check_vma=False)
```

```python
import functools

import jax
import jax.numpy as jnp
from jax import lax
from jax.experimental import pallas as pl
from jax.experimental.pallas import tpu as pltpu
from jax.sharding import PartitionSpec as P

CHANS = 16384
EPSILON = 1e-05
LANES = 128
CHUNKS = 4
WIDTHS = 9


def shifted(first, second, amount, inside):
    first = pltpu.roll(first, amount, 1)
    second = pltpu.roll(second, amount, 1)
    return jnp.where(inside, first, second), jnp.where(inside, second, 0.0)


def channel_kernel(x_hbm, mask_hbm, out_ref, xbuf, masks, sems, sums, squares, level2, rows32):
    beams, chans, samples = xbuf.shape
    step = chans // CHUNKS
    copies = []
    for k in range(CHUNKS):
        part = pl.ds(k * step, step)
        copies.append(pltpu.make_async_copy(x_hbm.at[:, part, :], xbuf.at[:, part, :], sems.at[k]))
        copies[-1].start()
    copies.append(pltpu.make_async_copy(mask_hbm, masks, sems.at[CHUNKS]))
    copies[-1].start()
    for k in range(CHUNKS):
        copies[k].wait()
        for c in range(k * step, (k + 1) * step, 16):
            total = square = None
            for b in range(beams):
                v = xbuf[b, c : c + 16, :].astype(jnp.float32)
                total = v if total is None else total + v
                square = v * v if square is None else square + v * v
            sums[c : c + 16, :] = total[:, :LANES] + total[:, LANES:]
            squares[c : c + 16, :] = square[:, :LANES] + square[:, LANES:]
    count = float(beams * samples)
    mean = jnp.sum(sums[...].T, axis=0, keepdims=True) / count
    var = jnp.sum(squares[...].T, axis=0, keepdims=True) / count - mean * mean
    copies[CHUNKS].wait()
    mask = masks[pl.ds(lax.axis_index("beam"), 1), :].astype(jnp.float32)
    scale = lax.rsqrt(var + EPSILON) * mask
    bands = chans // 4
    row = lax.broadcasted_iota(jnp.int32, (bands, chans), 0)
    chan = lax.broadcasted_iota(jnp.int32, (bands, chans), 1)
    weight = jnp.where(chan // 4 == row, scale, 0.0)
    high = weight.astype(jnp.bfloat16)
    rest = (weight - high.astype(jnp.float32)).astype(jnp.bfloat16)
    held = high.astype(jnp.float32) + rest.astype(jnp.float32)
    offset = jnp.sum(held * mean, axis=1, keepdims=True)
    both = jnp.concatenate([high, rest], axis=0)
    for b in range(beams):
        y = jnp.dot(both, xbuf[b], preferred_element_type=jnp.float32)
        y = y[:bands] + y[bands:] - offset
        level2[0, b * bands : (b + 1) * bands, :] = y[:, :LANES]
        level2[1, b * bands : (b + 1) * bands, :] = y[:, LANES:]
    lane = lax.broadcasted_iota(jnp.int32, (8, LANES), 1)

    def subband(tile, level, s):
        if level == 2:
            at = pl.ds(tile * 8 * bands + s, 8, stride=bands)
            return [(level2[0, at, :], level2[1, at, :])]
        low = subband(tile, level - 1, 2 * s)
        high = subband(tile, level - 1, 2 * s + 1)
        rows = []
        for r in range(len(low)):
            for shift in (r, r + 1):
                moved = high[r]
                if shift:
                    moved = shifted(*high[r], LANES - shift, lane < LANES - shift)
                rows.append((low[r][0] + moved[0], low[r][1] + moved[1]))
        return rows

    for tile in range(beams // 8):
        rows = subband(tile, 7, 0)
        for r, halves in enumerate(rows):
            for h in range(2):
                start = ((r // 4) * beams + tile * 8) * 8 + h * 4 + r % 4
                rows32[pl.ds(start, 8, stride=8), :] = halves[h]
    out_ref[...] = rows32[...].astype(jnp.bfloat16)


def trial_kernel(rows_ref, widths_hbm, out_ref, widths, sem, rows32, level11, trials, prefix):
    copy = pltpu.make_async_copy(widths_hbm, widths, sem)
    copy.start()
    f = lax.axis_index("freq")
    rows32[...] = rows_ref[...].astype(jnp.float32)
    lane = lax.broadcasted_iota(jnp.int32, (8, LANES), 1)
    sub = lax.broadcasted_iota(jnp.int32, (8, LANES), 0)
    upper = sub >= 4
    row = sub & 3

    pace = f * 4 + row
    begin = lane + jnp.where(upper, 64 * pace, 0)
    rows = []
    for u in range(64):
        here, there = u * 8, (u + 64) * 8
        first = jnp.where(upper, rows32[there - 4 : there + 4, :], rows32[here : here + 8, :])
        second = jnp.where(upper, rows32[there : there + 8, :], rows32[here + 4 : here + 12, :])
        time, begin = begin, begin + pace
        moved = time & (LANES - 1)
        inside = time < LANES
        first = jnp.take_along_axis(first, moved, axis=1, mode="promise_in_bounds")
        second = jnp.take_along_axis(second, moved, axis=1, mode="promise_in_bounds")
        first = jnp.where(inside, first, jnp.where(time < 2 * LANES, second, 0.0))
        rows.append((first, jnp.where(inside, second, 0.0)))

    def ahead(pair, s):
        return shifted(*pair, LANES - s, lane < LANES - s) if s else pair

    for k in range(6):
        width = 1 << k
        grown = []
        for u in range(32 >> k):
            for c in range(width):
                low = rows[2 * u * width + c]
                high = rows[2 * u * width + c + width]
                for e in range(2):
                    moved = ahead(high, c + e)
                    grown.append((low[0] + moved[0], low[1] + moved[1]))
        rows = grown
        if k == 3:
            for n, pair in enumerate(rows):
                for h in range(2):
                    level11[h, n * 8 : n * 8 + 8, :] = pair[h]
            rows = [tuple(level11[h, n * 8 : n * 8 + 8, :] for h in range(2)) for n in range(64)]

    for c in range(64):
        halves = [rows[c][h] for h in range(2)]
        turned = [pltpu.roll(v, 4, 0) for v in halves]
        pair = [jnp.where(upper, v, t) for v, t in zip(halves, turned)]
        time = lane + (sub >> 2) + c
        moved = time & (LANES - 1)
        inside = time < LANES
        first, second = (jnp.take_along_axis(v, moved, axis=1, mode="promise_in_bounds") for v in pair)
        moved = jnp.where(inside, first, second), jnp.where(inside, second, 0.0)
        for h in range(2):
            trials[h, c * 8 : c * 8 + 8, :] = jnp.where(upper, turned[h], halves[h]) + moved[h]

    count = trials.shape[1]
    samples = 2 * LANES
    span = prefix.shape[0] // 8
    parts = []
    for h in range(2):
        d = trials[h]
        high = d.astype(jnp.bfloat16)
        parts.append((high, (d - high.astype(jnp.float32)).astype(jnp.bfloat16)))
    values = jnp.concatenate([parts[0][0], parts[1][0], parts[0][1], parts[1][1]], axis=1)
    size = (samples + 16, 4 * LANES)
    step = lax.broadcasted_iota(jnp.int32, size, 0)
    time = lax.broadcasted_iota(jnp.int32, size, 1) & (samples - 1)
    lower = jnp.where(time < step, 1.0, 0.0).astype(jnp.bfloat16)
    summed = lax.dot_general(lower, values, (((1,), (1,)), ((), ())), preferred_element_type=jnp.float32)
    least = jnp.full((8, LANES), -jnp.inf, jnp.float32)
    for tile in range(count // LANES):
        for t in range(0, samples + 64, 8):
            part = least
            if t <= samples:
                part = summed[t : t + 8, tile * LANES : (tile + 1) * LANES]
            if t == samples:
                part = jnp.where(sub == 0, part, least)
            if t < span:
                prefix[pl.ds(t * 8 + tile, 8, stride=8), :] = part
            if t >= LANES:
                prefix[pl.ds((t - LANES) * 8 + 4 + tile, 8, stride=8), :] = part
    copy.wait()

    def boxcars(block, peaks):
        base = pl.multiple_of(block * 256, 256)
        starts = [prefix[pl.ds(base + t * 8, 8), :] for t in range(32)]
        out = []
        for k in range(WIDTHS):
            w = pl.multiple_of(base + widths[k] * 8, 8)
            two = [peaks[k], None]
            for n, start in enumerate(starts):
                box = prefix[pl.ds(w + n * 8, 8), :] - start
                two[n % 2] = box if two[n % 2] is None else jnp.maximum(two[n % 2], box)
            out.append(jnp.maximum(*two))
        return tuple(out)

    peaks = lax.fori_loop(0, 4, boxcars, (least,) * WIDTHS)
    best = least
    for k in range(WIDTHS):
        norm = lax.rsqrt(jnp.full((8, LANES), widths[k] * CHANS, jnp.int32).astype(jnp.float32))
        best = jnp.maximum(best, peaks[k] * norm)
    best = jnp.maximum(best, pltpu.roll(best, 4, 0))
    for i in range(count // LANES):
        place = (lane >> 1) * 8 + (lane & 1) * 4 + i
        found = jnp.take_along_axis(best, place & (LANES - 1), axis=1, mode="promise_in_bounds")
        found = jnp.where(sub == place // LANES, found, least)
        out_ref[:, i * LANES : (i + 1) * LANES] = jnp.max(found, axis=0, keepdims=True)


def in_hbm(array):
    return pltpu.with_memory_space_constraint(array, pltpu.HBM)


def shards(intensity, channel_mask, box_widths):
    beams, chans, samples = intensity.shape
    devices = lax.axis_size("beam") * lax.axis_size("freq")
    rows = pl.pallas_call(
        channel_kernel,
        out_shape=jax.ShapeDtypeStruct((devices * 8, LANES), jnp.bfloat16),
        in_specs=[pl.BlockSpec(memory_space=pltpu.HBM), pl.BlockSpec(memory_space=pltpu.HBM)],
        out_specs=pl.BlockSpec(memory_space=pltpu.VMEM),
        scratch_shapes=[
            pltpu.VMEM((beams, chans, samples), jnp.bfloat16),
            pltpu.VMEM((chans * lax.axis_size("beam") // LANES, LANES), jnp.int32),
            pltpu.SemaphoreType.DMA((CHUNKS + 1,)),
            pltpu.VMEM((chans, LANES), jnp.float32),
            pltpu.VMEM((chans, LANES), jnp.float32),
            pltpu.VMEM((2, beams * chans // 4, LANES), jnp.float32),
            pltpu.VMEM((devices * 8, LANES), jnp.float32),
        ],
        compiler_params=pltpu.CompilerParams(vmem_limit_bytes=32 * 1024 * 1024),
        name="channel_levels",
    )(in_hbm(intensity), in_hbm(channel_mask.reshape(-1, LANES)))
    rows = lax.all_to_all(rows.reshape(devices, 8, LANES), ("freq", "beam"), 0, 0, tiled=True)
    return pl.pallas_call(
        trial_kernel,
        out_shape=jax.ShapeDtypeStruct((1, 4 * LANES), jnp.float32),
        in_specs=[pl.BlockSpec(memory_space=pltpu.VMEM), pl.BlockSpec(memory_space=pltpu.HBM)],
        out_specs=pl.BlockSpec(memory_space=pltpu.VMEM),
        scratch_shapes=[
            pltpu.SMEM(box_widths.shape, jnp.int32),
            pltpu.SemaphoreType.DMA,
            pltpu.VMEM((devices * 8, LANES), jnp.float32),
            pltpu.VMEM((2, 512, LANES), jnp.float32),
            pltpu.VMEM((2, 512, LANES), jnp.float32),
            pltpu.VMEM((8 * (LANES + 64), LANES), jnp.float32),
        ],
        compiler_params=pltpu.CompilerParams(vmem_limit_bytes=32 * 1024 * 1024),
        name="trial_levels",
    )(rows.reshape(devices * 8, LANES), in_hbm(box_widths))


def solution(mesh):
    in_specs = (P(None, ("freq", "beam"), None), P("freq"), P())
    out_specs = P("beam", "freq")
    return jax.shard_map(shards, mesh=mesh, in_specs=in_specs, out_specs=out_specs, check_vma=False)
```

```python
import functools

import jax
import jax.numpy as jnp
from jax import lax
from jax.experimental import pallas as pl
from jax.experimental.pallas import tpu as pltpu
from jax.sharding import PartitionSpec as P

CHANS = 16384
EPSILON = 1e-05
LANES = 128
CHUNKS = 4
WIDTHS = 9


def shifted(first, second, amount, inside):
    first = pltpu.roll(first, amount, 1)
    second = pltpu.roll(second, amount, 1)
    return jnp.where(inside, first, second), jnp.where(inside, second, 0.0)


def channel_kernel(x_hbm, mask_hbm, out_ref, xbuf, masks, sems, sums, squares, level2, rows32):
    beams, chans, samples = xbuf.shape
    step = chans // CHUNKS
    copies = []
    for k in range(CHUNKS):
        part = pl.ds(k * step, step)
        copies.append(pltpu.make_async_copy(x_hbm.at[:, part, :], xbuf.at[:, part, :], sems.at[k]))
        copies[-1].start()
    copies.append(pltpu.make_async_copy(mask_hbm, masks, sems.at[CHUNKS]))
    copies[-1].start()
    for k in range(CHUNKS):
        copies[k].wait()
        for c in range(k * step, (k + 1) * step, 16):
            total = square = None
            for b in range(beams):
                v = xbuf[b, c : c + 16, :].astype(jnp.float32)
                total = v if total is None else total + v
                square = v * v if square is None else square + v * v
            sums[c : c + 16, :] = total[:, :LANES] + total[:, LANES:]
            squares[c : c + 16, :] = square[:, :LANES] + square[:, LANES:]
    count = float(beams * samples)
    mean = jnp.sum(sums[...].T, axis=0, keepdims=True) / count
    var = jnp.sum(squares[...].T, axis=0, keepdims=True) / count - mean * mean
    copies[CHUNKS].wait()
    mask = masks[pl.ds(lax.axis_index("beam"), 1), :].astype(jnp.float32)
    scale = lax.rsqrt(var + EPSILON) * mask
    bands = chans // 4
    row = lax.broadcasted_iota(jnp.int32, (bands, chans), 0)
    chan = lax.broadcasted_iota(jnp.int32, (bands, chans), 1)
    weight = jnp.where(chan // 4 == row, scale, 0.0)
    high = weight.astype(jnp.bfloat16)
    rest = (weight - high.astype(jnp.float32)).astype(jnp.bfloat16)
    held = high.astype(jnp.float32) + rest.astype(jnp.float32)
    offset = jnp.sum(held * mean, axis=1, keepdims=True)
    both = jnp.concatenate([high, rest], axis=0)
    for b in range(beams):
        y = jnp.dot(both, xbuf[b], preferred_element_type=jnp.float32)
        y = y[:bands] + y[bands:] - offset
        level2[0, b * bands : (b + 1) * bands, :] = y[:, :LANES]
        level2[1, b * bands : (b + 1) * bands, :] = y[:, LANES:]
    lane = lax.broadcasted_iota(jnp.int32, (8, LANES), 1)

    def subband(tile, level, s):
        if level == 2:
            at = pl.ds(tile * 8 * bands + s, 8, stride=bands)
            return [(level2[0, at, :], level2[1, at, :])]
        low = subband(tile, level - 1, 2 * s)
        high = subband(tile, level - 1, 2 * s + 1)
        rows = []
        for r in range(len(low)):
            for shift in (r, r + 1):
                moved = high[r]
                if shift:
                    moved = shifted(*high[r], LANES - shift, lane < LANES - shift)
                rows.append((low[r][0] + moved[0], low[r][1] + moved[1]))
        return rows

    for tile in range(beams // 8):
        rows = subband(tile, 7, 0)
        for r, halves in enumerate(rows):
            for h in range(2):
                start = ((r // 4) * beams + tile * 8) * 8 + h * 4 + r % 4
                rows32[pl.ds(start, 8, stride=8), :] = halves[h]
    out_ref[...] = rows32[...].astype(jnp.bfloat16)


def trial_kernel(rows_ref, widths_hbm, out_ref, widths, sem, rows32, trials, prefix):
    copy = pltpu.make_async_copy(widths_hbm, widths, sem)
    copy.start()
    f = lax.axis_index("freq")
    rows32[...] = rows_ref[...].astype(jnp.float32)
    lane = lax.broadcasted_iota(jnp.int32, (8, LANES), 1)
    sub = lax.broadcasted_iota(jnp.int32, (8, LANES), 0)
    upper = sub >= 4
    row = sub & 3

    pace = f * 4 + row
    begin = lane + jnp.where(upper, 64 * pace, 0)
    rows = []
    for u in range(64):
        here, there = u * 8, (u + 64) * 8
        first = jnp.where(upper, rows32[there - 4 : there + 4, :], rows32[here : here + 8, :])
        second = jnp.where(upper, rows32[there : there + 8, :], rows32[here + 4 : here + 12, :])
        time, begin = begin, begin + pace
        moved = time & (LANES - 1)
        inside = time < LANES
        first = jnp.take_along_axis(first, moved, axis=1, mode="promise_in_bounds")
        second = jnp.take_along_axis(second, moved, axis=1, mode="promise_in_bounds")
        first = jnp.where(inside, first, jnp.where(time < 2 * LANES, second, 0.0))
        rows.append((first, jnp.where(inside, second, 0.0)))

    def ahead(pair, s):
        return shifted(*pair, LANES - s, lane < LANES - s) if s else pair

    for k in range(6):
        width = 1 << k
        grown = []
        for u in range(32 >> k):
            for c in range(width):
                low = rows[2 * u * width + c]
                high = rows[2 * u * width + c + width]
                for e in range(2):
                    moved = ahead(high, c + e)
                    grown.append((low[0] + moved[0], low[1] + moved[1]))
        rows = grown

    for c in range(64):
        halves = [rows[c][h] for h in range(2)]
        turned = [pltpu.roll(v, 4, 0) for v in halves]
        pair = [jnp.where(upper, v, t) for v, t in zip(halves, turned)]
        time = lane + (sub >> 2) + c
        moved = time & (LANES - 1)
        inside = time < LANES
        first, second = (jnp.take_along_axis(v, moved, axis=1, mode="promise_in_bounds") for v in pair)
        moved = jnp.where(inside, first, second), jnp.where(inside, second, 0.0)
        for h in range(2):
            trials[h, c * 8 : c * 8 + 8, :] = jnp.where(upper, turned[h], halves[h]) + moved[h]

    count = trials.shape[1]
    samples = 2 * LANES
    span = prefix.shape[0] // 8
    parts = []
    for h in range(2):
        d = trials[h]
        high = d.astype(jnp.bfloat16)
        parts.append((high, (d - high.astype(jnp.float32)).astype(jnp.bfloat16)))
    values = jnp.concatenate([parts[0][0], parts[1][0], parts[0][1], parts[1][1]], axis=1)
    size = (samples + 16, 4 * LANES)
    step = lax.broadcasted_iota(jnp.int32, size, 0)
    time = lax.broadcasted_iota(jnp.int32, size, 1) & (samples - 1)
    lower = jnp.where(time < step, 1.0, 0.0).astype(jnp.bfloat16)
    summed = lax.dot_general(lower, values, (((1,), (1,)), ((), ())), preferred_element_type=jnp.float32)
    least = jnp.full((8, LANES), -jnp.inf, jnp.float32)
    for tile in range(count // LANES):
        for t in range(0, samples + 64, 8):
            part = least
            if t <= samples:
                part = summed[t : t + 8, tile * LANES : (tile + 1) * LANES]
            if t == samples:
                part = jnp.where(sub == 0, part, least)
            if t < span:
                prefix[pl.ds(t * 8 + tile, 8, stride=8), :] = part
            if t >= LANES:
                prefix[pl.ds((t - LANES) * 8 + 4 + tile, 8, stride=8), :] = part
    copy.wait()

    def boxcars(block, peaks):
        base = block * 256
        starts = [prefix[pl.ds(base + t * 8, 8), :] for t in range(32)]
        out = []
        for k in range(WIDTHS):
            w = pl.multiple_of(base + widths[k] * 8, 8)
            two = [peaks[k], None]
            for n, start in enumerate(starts):
                box = prefix[pl.ds(w + n * 8, 8), :] - start
                two[n % 2] = box if two[n % 2] is None else jnp.maximum(two[n % 2], box)
            out.append(jnp.maximum(*two))
        return tuple(out)

    peaks = (least,) * WIDTHS
    for block in range(4):
        peaks = boxcars(block, peaks)
    best = least
    for k in range(WIDTHS):
        norm = lax.rsqrt(jnp.full((8, LANES), widths[k] * CHANS, jnp.int32).astype(jnp.float32))
        best = jnp.maximum(best, peaks[k] * norm)
    best = jnp.maximum(best, pltpu.roll(best, 4, 0))
    for i in range(count // LANES):
        place = (lane >> 1) * 8 + (lane & 1) * 4 + i
        found = jnp.take_along_axis(best, place & (LANES - 1), axis=1, mode="promise_in_bounds")
        found = jnp.where(sub == place // LANES, found, least)
        out_ref[:, i * LANES : (i + 1) * LANES] = jnp.max(found, axis=0, keepdims=True)


def in_hbm(array):
    return pltpu.with_memory_space_constraint(array, pltpu.HBM)


def shards(intensity, channel_mask, box_widths):
    beams, chans, samples = intensity.shape
    devices = lax.axis_size("beam") * lax.axis_size("freq")
    rows = pl.pallas_call(
        channel_kernel,
        out_shape=jax.ShapeDtypeStruct((devices * 8, LANES), jnp.bfloat16),
        in_specs=[pl.BlockSpec(memory_space=pltpu.HBM), pl.BlockSpec(memory_space=pltpu.HBM)],
        out_specs=pl.BlockSpec(memory_space=pltpu.VMEM),
        scratch_shapes=[
            pltpu.VMEM((beams, chans, samples), jnp.bfloat16),
            pltpu.VMEM((chans * lax.axis_size("beam") // LANES, LANES), jnp.int32),
            pltpu.SemaphoreType.DMA((CHUNKS + 1,)),
            pltpu.VMEM((chans, LANES), jnp.float32),
            pltpu.VMEM((chans, LANES), jnp.float32),
            pltpu.VMEM((2, beams * chans // 4, LANES), jnp.float32),
            pltpu.VMEM((devices * 8, LANES), jnp.float32),
        ],
        compiler_params=pltpu.CompilerParams(vmem_limit_bytes=32 * 1024 * 1024),
        name="channel_levels",
    )(in_hbm(intensity), in_hbm(channel_mask.reshape(-1, LANES)))
    rows = lax.all_to_all(rows.reshape(devices, 8, LANES), ("freq", "beam"), 0, 0, tiled=True)
    return pl.pallas_call(
        trial_kernel,
        out_shape=jax.ShapeDtypeStruct((1, 4 * LANES), jnp.float32),
        in_specs=[pl.BlockSpec(memory_space=pltpu.VMEM), pl.BlockSpec(memory_space=pltpu.HBM)],
        out_specs=pl.BlockSpec(memory_space=pltpu.VMEM),
        scratch_shapes=[
            pltpu.SMEM(box_widths.shape, jnp.int32),
            pltpu.SemaphoreType.DMA,
            pltpu.VMEM((devices * 8, LANES), jnp.float32),
            pltpu.VMEM((2, 512, LANES), jnp.float32),
            pltpu.VMEM((8 * (LANES + 64), LANES), jnp.float32),
        ],
        compiler_params=pltpu.CompilerParams(vmem_limit_bytes=32 * 1024 * 1024),
        name="trial_levels",
    )(rows.reshape(devices * 8, LANES), in_hbm(box_widths))


def solution(mesh):
    in_specs = (P(None, ("freq", "beam"), None), P("freq"), P())
    out_specs = P("beam", "freq")
    return jax.shard_map(shards, mesh=mesh, in_specs=in_specs, out_specs=out_specs, check_vma=False)
```

```python
import functools

import jax
import jax.numpy as jnp
from jax import lax
from jax.experimental import pallas as pl
from jax.experimental.pallas import tpu as pltpu
from jax.sharding import PartitionSpec as P

CHANS = 16384
EPSILON = 1e-05
LANES = 128
CHUNKS = 4
WIDTHS = 9


def shifted(first, second, amount, inside):
    first = pltpu.roll(first, amount, 1)
    second = pltpu.roll(second, amount, 1)
    return jnp.where(inside, first, second), jnp.where(inside, second, 0.0)


def channel_kernel(x_hbm, mask_hbm, out_ref, xbuf, masks, sems, sums, squares, level2, rows32):
    beams, chans, samples = xbuf.shape
    step = chans // CHUNKS
    copies = []
    for k in range(CHUNKS):
        part = pl.ds(k * step, step)
        copies.append(pltpu.make_async_copy(x_hbm.at[:, part, :], xbuf.at[:, part, :], sems.at[k]))
        copies[-1].start()
    copies.append(pltpu.make_async_copy(mask_hbm, masks, sems.at[CHUNKS]))
    copies[-1].start()
    for k in range(CHUNKS):
        copies[k].wait()
        for c in range(k * step, (k + 1) * step, 16):
            total = square = None
            for b in range(beams):
                v = xbuf[b, c : c + 16, :].astype(jnp.float32)
                total = v if total is None else total + v
                square = v * v if square is None else square + v * v
            sums[c : c + 16, :] = total[:, :LANES] + total[:, LANES:]
            squares[c : c + 16, :] = square[:, :LANES] + square[:, LANES:]
    count = float(beams * samples)
    mean = jnp.sum(sums[...].T, axis=0, keepdims=True) / count
    var = jnp.sum(squares[...].T, axis=0, keepdims=True) / count - mean * mean
    copies[CHUNKS].wait()
    mask = masks[pl.ds(lax.axis_index("beam"), 1), :].astype(jnp.float32)
    scale = lax.rsqrt(var + EPSILON) * mask
    bands = chans // 4
    row = lax.broadcasted_iota(jnp.int32, (bands, chans), 0)
    chan = lax.broadcasted_iota(jnp.int32, (bands, chans), 1)
    weight = jnp.where(chan // 4 == row, scale, 0.0)
    high = weight.astype(jnp.bfloat16)
    rest = (weight - high.astype(jnp.float32)).astype(jnp.bfloat16)
    held = high.astype(jnp.float32) + rest.astype(jnp.float32)
    offset = jnp.sum(held * mean, axis=1, keepdims=True)
    both = jnp.concatenate([high, rest], axis=0)
    for b in range(beams):
        y = jnp.dot(both, xbuf[b], preferred_element_type=jnp.float32)
        y = y[:bands] + y[bands:] - offset
        level2[0, b * bands : (b + 1) * bands, :] = y[:, :LANES]
        level2[1, b * bands : (b + 1) * bands, :] = y[:, LANES:]
    lane = lax.broadcasted_iota(jnp.int32, (8, LANES), 1)

    def subband(tile, level, s):
        if level == 2:
            at = pl.ds(tile * 8 * bands + s, 8, stride=bands)
            return [(level2[0, at, :], level2[1, at, :])]
        low = subband(tile, level - 1, 2 * s)
        high = subband(tile, level - 1, 2 * s + 1)
        rows = []
        for r in range(len(low)):
            for shift in (r, r + 1):
                moved = high[r]
                if shift:
                    moved = shifted(*high[r], LANES - shift, lane < LANES - shift)
                rows.append((low[r][0] + moved[0], low[r][1] + moved[1]))
        return rows

    for tile in range(beams // 8):
        rows = subband(tile, 7, 0)
        for r, halves in enumerate(rows):
            for h in range(2):
                start = ((r // 4) * beams + tile * 8) * 8 + h * 4 + r % 4
                rows32[pl.ds(start, 8, stride=8), :] = halves[h]
    out_ref[...] = rows32[...].astype(jnp.bfloat16)


def trial_kernel(rows_ref, widths_hbm, out_ref, widths, sem, rows32, level11, trials, prefix):
    copy = pltpu.make_async_copy(widths_hbm, widths, sem)
    copy.start()
    f = lax.axis_index("freq")
    rows32[...] = rows_ref[...].astype(jnp.float32)
    lane = lax.broadcasted_iota(jnp.int32, (8, LANES), 1)
    sub = lax.broadcasted_iota(jnp.int32, (8, LANES), 0)
    upper = sub >= 4
    row = sub & 3

    pace = f * 4 + row
    begin = lane + jnp.where(upper, 64 * pace, 0)
    rows = []
    for u in range(64):
        here, there = u * 8, (u + 64) * 8
        first = jnp.where(upper, rows32[there - 4 : there + 4, :], rows32[here : here + 8, :])
        second = jnp.where(upper, rows32[there : there + 8, :], rows32[here + 4 : here + 12, :])
        time, begin = begin, begin + pace
        moved = time & (LANES - 1)
        inside = time < LANES
        first = jnp.take_along_axis(first, moved, axis=1, mode="promise_in_bounds")
        second = jnp.take_along_axis(second, moved, axis=1, mode="promise_in_bounds")
        first = jnp.where(inside, first, jnp.where(time < 2 * LANES, second, 0.0))
        rows.append((first, jnp.where(inside, second, 0.0)))

    def ahead(pair, s):
        return shifted(*pair, LANES - s, lane < LANES - s) if s else pair

    for k in range(6):
        width = 1 << k
        grown = []
        for u in range(32 >> k):
            for c in range(width):
                low = rows[2 * u * width + c]
                high = rows[2 * u * width + c + width]
                for e in range(2):
                    moved = ahead(high, c + e)
                    grown.append((low[0] + moved[0], low[1] + moved[1]))
        rows = grown
        if k == 3:
            for n, pair in enumerate(rows):
                for h in range(2):
                    level11[h, n * 8 : n * 8 + 8, :] = pair[h]
            rows = [tuple(level11[h, n * 8 : n * 8 + 8, :] for h in range(2)) for n in range(64)]

    for c in range(64):
        halves = [rows[c][h] for h in range(2)]
        turned = [pltpu.roll(v, 4, 0) for v in halves]
        pair = [jnp.where(upper, v, t) for v, t in zip(halves, turned)]
        time = lane + (sub >> 2) + c
        moved = time & (LANES - 1)
        inside = time < LANES
        first, second = (jnp.take_along_axis(v, moved, axis=1, mode="promise_in_bounds") for v in pair)
        moved = jnp.where(inside, first, second), jnp.where(inside, second, 0.0)
        for h in range(2):
            trials[h, c * 8 : c * 8 + 8, :] = jnp.where(upper, turned[h], halves[h]) + moved[h]

    count = trials.shape[1]
    samples = 2 * LANES
    span = prefix.shape[0] // 8
    parts = []
    for h in range(2):
        d = trials[h]
        high = d.astype(jnp.bfloat16)
        parts.append((high, (d - high.astype(jnp.float32)).astype(jnp.bfloat16)))
    values = jnp.concatenate([*parts[0], *parts[1]], axis=1)
    size = (samples + 16, 4 * LANES)
    step = lax.broadcasted_iota(jnp.int32, size, 0)
    time = lax.broadcasted_iota(jnp.int32, size, 1)
    time = (time & (LANES - 1)) + time // samples * LANES
    lower = jnp.where(time < step, 1.0, 0.0).astype(jnp.bfloat16)
    both = (((1,), (1,)), ((), ()))
    summed = jnp.concatenate([
        lax.dot_general(lower[:LANES, :samples], values[:, :samples], both, preferred_element_type=jnp.float32),
        lax.dot_general(lower[LANES:], values, both, preferred_element_type=jnp.float32),
    ])
    least = jnp.full((8, LANES), -jnp.inf, jnp.float32)
    for tile in range(count // LANES):
        for t in range(0, samples + 64, 8):
            part = least
            if t <= samples:
                part = summed[t : t + 8, tile * LANES : (tile + 1) * LANES]
            if t == samples:
                part = jnp.where(sub == 0, part, least)
            if t < span:
                prefix[pl.ds(t * 8 + tile, 8, stride=8), :] = part
            if t >= LANES:
                prefix[pl.ds((t - LANES) * 8 + 4 + tile, 8, stride=8), :] = part
    copy.wait()

    def boxcars(block, peaks):
        base = pl.multiple_of(block * 256, 256)
        starts = [prefix[pl.ds(base + t * 8, 8), :] for t in range(32)]
        out = []
        for k in range(WIDTHS):
            w = pl.multiple_of(base + widths[k] * 8, 8)
            two = [peaks[k], None]
            for n, start in enumerate(starts):
                box = prefix[pl.ds(w + n * 8, 8), :] - start
                two[n % 2] = box if two[n % 2] is None else jnp.maximum(two[n % 2], box)
            out.append(jnp.maximum(*two))
        return tuple(out)

    peaks = lax.fori_loop(0, 4, boxcars, (least,) * WIDTHS)
    best = least
    for k in range(WIDTHS):
        norm = lax.rsqrt(jnp.full((8, LANES), widths[k] * CHANS, jnp.int32).astype(jnp.float32))
        best = jnp.maximum(best, peaks[k] * norm)
    best = jnp.maximum(best, pltpu.roll(best, 4, 0))
    for i in range(count // LANES):
        place = (lane >> 1) * 8 + (lane & 1) * 4 + i
        found = jnp.take_along_axis(best, place & (LANES - 1), axis=1, mode="promise_in_bounds")
        found = jnp.where(sub == place // LANES, found, least)
        out_ref[:, i * LANES : (i + 1) * LANES] = jnp.max(found, axis=0, keepdims=True)


def in_hbm(array):
    return pltpu.with_memory_space_constraint(array, pltpu.HBM)


def shards(intensity, channel_mask, box_widths):
    beams, chans, samples = intensity.shape
    devices = lax.axis_size("beam") * lax.axis_size("freq")
    rows = pl.pallas_call(
        channel_kernel,
        out_shape=jax.ShapeDtypeStruct((devices * 8, LANES), jnp.bfloat16),
        in_specs=[pl.BlockSpec(memory_space=pltpu.HBM), pl.BlockSpec(memory_space=pltpu.HBM)],
        out_specs=pl.BlockSpec(memory_space=pltpu.VMEM),
        scratch_shapes=[
            pltpu.VMEM((beams, chans, samples), jnp.bfloat16),
            pltpu.VMEM((chans * lax.axis_size("beam") // LANES, LANES), jnp.int32),
            pltpu.SemaphoreType.DMA((CHUNKS + 1,)),
            pltpu.VMEM((chans, LANES), jnp.float32),
            pltpu.VMEM((chans, LANES), jnp.float32),
            pltpu.VMEM((2, beams * chans // 4, LANES), jnp.float32),
            pltpu.VMEM((devices * 8, LANES), jnp.float32),
        ],
        compiler_params=pltpu.CompilerParams(vmem_limit_bytes=32 * 1024 * 1024),
        name="channel_levels",
    )(in_hbm(intensity), in_hbm(channel_mask.reshape(-1, LANES)))
    rows = lax.all_to_all(rows.reshape(devices, 8, LANES), ("freq", "beam"), 0, 0, tiled=True)
    return pl.pallas_call(
        trial_kernel,
        out_shape=jax.ShapeDtypeStruct((1, 4 * LANES), jnp.float32),
        in_specs=[pl.BlockSpec(memory_space=pltpu.VMEM), pl.BlockSpec(memory_space=pltpu.HBM)],
        out_specs=pl.BlockSpec(memory_space=pltpu.VMEM),
        scratch_shapes=[
            pltpu.SMEM(box_widths.shape, jnp.int32),
            pltpu.SemaphoreType.DMA,
            pltpu.VMEM((devices * 8, LANES), jnp.float32),
            pltpu.VMEM((2, 512, LANES), jnp.float32),
            pltpu.VMEM((2, 512, LANES), jnp.float32),
            pltpu.VMEM((8 * (LANES + 64), LANES), jnp.float32),
        ],
        compiler_params=pltpu.CompilerParams(vmem_limit_bytes=32 * 1024 * 1024),
        name="trial_levels",
    )(rows.reshape(devices * 8, LANES), in_hbm(box_widths))


def solution(mesh):
    in_specs = (P(None, ("freq", "beam"), None), P("freq"), P())
    out_specs = P("beam", "freq")
    return jax.shard_map(shards, mesh=mesh, in_specs=in_specs, out_specs=out_specs, check_vma=False)
```

```python
import functools

import jax
import jax.numpy as jnp
from jax import lax
from jax.experimental import pallas as pl
from jax.experimental.pallas import tpu as pltpu
from jax.sharding import PartitionSpec as P

CHANS = 16384
EPSILON = 1e-05
LANES = 128
CHUNKS = 4
WIDTHS = 9


def shifted(first, second, amount, inside):
    first = pltpu.roll(first, amount, 1)
    second = pltpu.roll(second, amount, 1)
    return jnp.where(inside, first, second), jnp.where(inside, second, 0.0)


def channel_kernel(x_hbm, mask_hbm, out_ref, xbuf, masks, sems, sums, squares, level2, rows32):
    beams, chans, samples = xbuf.shape
    step = chans // CHUNKS
    copies = []
    for k in range(CHUNKS):
        part = pl.ds(k * step, step)
        copies.append(pltpu.make_async_copy(x_hbm.at[:, part, :], xbuf.at[:, part, :], sems.at[k]))
        copies[-1].start()
    copies.append(pltpu.make_async_copy(mask_hbm, masks, sems.at[CHUNKS]))
    copies[-1].start()
    for k in range(CHUNKS):
        copies[k].wait()
        for c in range(k * step, (k + 1) * step, 16):
            total = square = None
            for b in range(beams):
                v = xbuf[b, c : c + 16, :].astype(jnp.float32)
                total = v if total is None else total + v
                square = v * v if square is None else square + v * v
            sums[c : c + 16, :] = total[:, :LANES] + total[:, LANES:]
            squares[c : c + 16, :] = square[:, :LANES] + square[:, LANES:]
    count = float(beams * samples)
    mean = jnp.sum(sums[...].T, axis=0, keepdims=True) / count
    var = jnp.sum(squares[...].T, axis=0, keepdims=True) / count - mean * mean
    copies[CHUNKS].wait()
    mask = masks[pl.ds(lax.axis_index("beam"), 1), :].astype(jnp.float32)
    scale = lax.rsqrt(var + EPSILON) * mask
    bands = chans // 4
    row = lax.broadcasted_iota(jnp.int32, (bands, chans), 0)
    chan = lax.broadcasted_iota(jnp.int32, (bands, chans), 1)
    weight = jnp.where(chan // 4 == row, scale, 0.0)
    high = weight.astype(jnp.bfloat16)
    rest = (weight - high.astype(jnp.float32)).astype(jnp.bfloat16)
    held = high.astype(jnp.float32) + rest.astype(jnp.float32)
    offset = jnp.sum(held * mean, axis=1, keepdims=True)
    both = jnp.concatenate([high, rest], axis=0)
    for b in range(beams):
        y = jnp.dot(both, xbuf[b], preferred_element_type=jnp.float32)
        y = y[:bands] + y[bands:] - offset
        level2[0, b * bands : (b + 1) * bands, :] = y[:, :LANES]
        level2[1, b * bands : (b + 1) * bands, :] = y[:, LANES:]
    lane = lax.broadcasted_iota(jnp.int32, (8, LANES), 1)

    def subband(tile, level, s):
        if level == 2:
            at = pl.ds(tile * 8 * bands + s, 8, stride=bands)
            return [(level2[0, at, :], level2[1, at, :])]
        low = subband(tile, level - 1, 2 * s)
        high = subband(tile, level - 1, 2 * s + 1)
        rows = []
        for r in range(len(low)):
            for shift in (r, r + 1):
                moved = high[r]
                if shift:
                    moved = shifted(*high[r], LANES - shift, lane < LANES - shift)
                rows.append((low[r][0] + moved[0], low[r][1] + moved[1]))
        return rows

    for tile in range(beams // 8):
        rows = subband(tile, 7, 0)
        for r, halves in enumerate(rows):
            for h in range(2):
                start = ((r // 4) * beams + tile * 8) * 8 + h * 4 + r % 4
                rows32[pl.ds(start, 8, stride=8), :] = halves[h]
    out_ref[...] = rows32[...].astype(jnp.bfloat16)


def trial_kernel(rows_ref, widths_hbm, out_ref, widths, sem, rows32, level11, trials, prefix):
    copy = pltpu.make_async_copy(widths_hbm, widths, sem)
    copy.start()
    f = lax.axis_index("freq")
    rows32[...] = rows_ref[...].astype(jnp.float32)
    lane = lax.broadcasted_iota(jnp.int32, (8, LANES), 1)
    sub = lax.broadcasted_iota(jnp.int32, (8, LANES), 0)
    upper = sub >= 4
    row = sub & 3

    pace = f * 4 + row
    begin = lane + jnp.where(upper, 64 * pace, 0)
    rows = []
    for u in range(64):
        here, there = u * 8, (u + 64) * 8
        first = jnp.where(upper, rows32[there - 4 : there + 4, :], rows32[here : here + 8, :])
        second = jnp.where(upper, rows32[there : there + 8, :], rows32[here + 4 : here + 12, :])
        time, begin = begin, begin + pace
        moved = time & (LANES - 1)
        inside = time < LANES
        first = jnp.take_along_axis(first, moved, axis=1, mode="promise_in_bounds")
        second = jnp.take_along_axis(second, moved, axis=1, mode="promise_in_bounds")
        first = jnp.where(inside, first, jnp.where(time < 2 * LANES, second, 0.0))
        rows.append((first, jnp.where(inside, second, 0.0)))

    def ahead(pair, s):
        return shifted(*pair, LANES - s, lane < LANES - s) if s else pair

    for k in range(6):
        width = 1 << k
        grown = [None] * 64
        for c in range(width):
            for u in range(32 >> k):
                low = rows[2 * u * width + c]
                high = rows[2 * u * width + c + width]
                for e in range(2):
                    moved = ahead(high, c + e)
                    grown[2 * u * width + 2 * c + e] = (low[0] + moved[0], low[1] + moved[1])
        rows = grown
        if k == 3:
            for n, pair in enumerate(rows):
                for h in range(2):
                    level11[h, n * 8 : n * 8 + 8, :] = pair[h]
            rows = [tuple(level11[h, n * 8 : n * 8 + 8, :] for h in range(2)) for n in range(64)]

    for c in range(64):
        halves = [rows[c][h] for h in range(2)]
        turned = [pltpu.roll(v, 4, 0) for v in halves]
        pair = [jnp.where(upper, v, t) for v, t in zip(halves, turned)]
        time = lane + (sub >> 2) + c
        moved = time & (LANES - 1)
        inside = time < LANES
        first, second = (jnp.take_along_axis(v, moved, axis=1, mode="promise_in_bounds") for v in pair)
        moved = jnp.where(inside, first, second), jnp.where(inside, second, 0.0)
        for h in range(2):
            trials[h, c * 8 : c * 8 + 8, :] = jnp.where(upper, turned[h], halves[h]) + moved[h]

    count = trials.shape[1]
    samples = 2 * LANES
    span = prefix.shape[0] // 8
    parts = []
    for h in range(2):
        d = trials[h]
        high = d.astype(jnp.bfloat16)
        parts.append((high, (d - high.astype(jnp.float32)).astype(jnp.bfloat16)))
    values = jnp.concatenate([parts[0][0], parts[1][0], parts[0][1], parts[1][1]], axis=1)
    size = (samples + 16, 4 * LANES)
    step = lax.broadcasted_iota(jnp.int32, size, 0)
    time = lax.broadcasted_iota(jnp.int32, size, 1) & (samples - 1)
    lower = jnp.where(time < step, 1.0, 0.0).astype(jnp.bfloat16)
    summed = lax.dot_general(lower, values, (((1,), (1,)), ((), ())), preferred_element_type=jnp.float32)
    least = jnp.full((8, LANES), -jnp.inf, jnp.float32)
    for tile in range(count // LANES):
        for t in range(0, samples + 64, 8):
            part = least
            if t <= samples:
                part = summed[t : t + 8, tile * LANES : (tile + 1) * LANES]
            if t == samples:
                part = jnp.where(sub == 0, part, least)
            if t < span:
                prefix[pl.ds(t * 8 + tile, 8, stride=8), :] = part
            if t >= LANES:
                prefix[pl.ds((t - LANES) * 8 + 4 + tile, 8, stride=8), :] = part
    copy.wait()

    def boxcars(block, peaks):
        base = block * 256
        starts = [prefix[pl.ds(base + t * 8, 8), :] for t in range(32)]
        out = []
        for k in range(WIDTHS):
            w = pl.multiple_of(base + widths[k] * 8, 8)
            two = [peaks[k], None]
            for n, start in enumerate(starts):
                box = prefix[pl.ds(w + n * 8, 8), :] - start
                two[n % 2] = box if two[n % 2] is None else jnp.maximum(two[n % 2], box)
            out.append(jnp.maximum(*two))
        return tuple(out)

    peaks = (least,) * WIDTHS
    for block in range(4):
        peaks = boxcars(block, peaks)
    best = least
    for k in range(WIDTHS):
        norm = lax.rsqrt(jnp.full((8, LANES), widths[k] * CHANS, jnp.int32).astype(jnp.float32))
        best = jnp.maximum(best, peaks[k] * norm)
    best = jnp.maximum(best, pltpu.roll(best, 4, 0))
    for i in range(count // LANES):
        place = (lane >> 1) * 8 + (lane & 1) * 4 + i
        found = jnp.take_along_axis(best, place & (LANES - 1), axis=1, mode="promise_in_bounds")
        found = jnp.where(sub == place // LANES, found, least)
        out_ref[:, i * LANES : (i + 1) * LANES] = jnp.max(found, axis=0, keepdims=True)


def in_hbm(array):
    return pltpu.with_memory_space_constraint(array, pltpu.HBM)


def shards(intensity, channel_mask, box_widths):
    beams, chans, samples = intensity.shape
    devices = lax.axis_size("beam") * lax.axis_size("freq")
    rows = pl.pallas_call(
        channel_kernel,
        out_shape=jax.ShapeDtypeStruct((devices * 8, LANES), jnp.bfloat16),
        in_specs=[pl.BlockSpec(memory_space=pltpu.HBM), pl.BlockSpec(memory_space=pltpu.HBM)],
        out_specs=pl.BlockSpec(memory_space=pltpu.VMEM),
        scratch_shapes=[
            pltpu.VMEM((beams, chans, samples), jnp.bfloat16),
            pltpu.VMEM((chans * lax.axis_size("beam") // LANES, LANES), jnp.int32),
            pltpu.SemaphoreType.DMA((CHUNKS + 1,)),
            pltpu.VMEM((chans, LANES), jnp.float32),
            pltpu.VMEM((chans, LANES), jnp.float32),
            pltpu.VMEM((2, beams * chans // 4, LANES), jnp.float32),
            pltpu.VMEM((devices * 8, LANES), jnp.float32),
        ],
        compiler_params=pltpu.CompilerParams(vmem_limit_bytes=32 * 1024 * 1024),
        name="channel_levels",
    )(in_hbm(intensity), in_hbm(channel_mask.reshape(-1, LANES)))
    rows = lax.all_to_all(rows.reshape(devices, 8, LANES), ("freq", "beam"), 0, 0, tiled=True)
    return pl.pallas_call(
        trial_kernel,
        out_shape=jax.ShapeDtypeStruct((1, 4 * LANES), jnp.float32),
        in_specs=[pl.BlockSpec(memory_space=pltpu.VMEM), pl.BlockSpec(memory_space=pltpu.HBM)],
        out_specs=pl.BlockSpec(memory_space=pltpu.VMEM),
        scratch_shapes=[
            pltpu.SMEM(box_widths.shape, jnp.int32),
            pltpu.SemaphoreType.DMA,
            pltpu.VMEM((devices * 8, LANES), jnp.float32),
            pltpu.VMEM((2, 512, LANES), jnp.float32),
            pltpu.VMEM((2, 512, LANES), jnp.float32),
            pltpu.VMEM((8 * (LANES + 64), LANES), jnp.float32),
        ],
        compiler_params=pltpu.CompilerParams(vmem_limit_bytes=32 * 1024 * 1024),
        name="trial_levels",
    )(rows.reshape(devices * 8, LANES), in_hbm(box_widths))


def solution(mesh):
    in_specs = (P(None, ("freq", "beam"), None), P("freq"), P())
    out_specs = P("beam", "freq")
    return jax.shard_map(shards, mesh=mesh, in_specs=in_specs, out_specs=out_specs, check_vma=False)
```
